32 devices in a mesh: gx: 8 (over z, y), gy: 4 (over x, core).
Axes of the slice: x: 2, y: 2, z: 4, core: 2. Of those that a mesh axis runs over, the one named last changes fastest.
Arguments:
- increment: float32 [1, 90, 384, 512], P(None, None, 'gx', 'gy'), may hold values from -6 to 6
- covariances: float32 [19, 90, 90], replicated, may hold values from 0 to 8, as said below
Outputs:
- weighted: float32 [1, 90, 384, 512], P(None, None, 'gx', 'gy')
The draws below stay inside these ranges and needn't reach their ends.
Inputs may be any that keep to these rules, and one draw needn't show every extreme that they name: `covariances`: one matrix of order 90 for each subband, of order one up to a factor that grows with the subband's level.
All inputs are finite; a program needn't handle non-finite values.
Results may differ from the reference program's by a relative error of at most 0.0001.
Values sent between devices are 32-bit elements; how exact they have to be, the bound alone decides.
A program may use at most 128 MiB of HBM per device.

```python
import math
import jax
import jax.numpy as jnp
from jax import lax

MEMBERS = 1
NZ = 90
LEVELS = 6
SUBBANDS = 19
NX = 384
NY = 512


def draw_covariances(key, part):
    key = jax.random.fold_in(key, 11)
    key_length, key_raw, key_diag = jax.random.split(key, 3)
    heights = jnp.arange(NZ, dtype=jnp.float32)
    distance = jnp.abs(heights[:, None] - heights[None, :])
    lengths = jnp.exp(jax.random.uniform(key_length, (SUBBANDS, 1, 1), jnp.float32, math.log(2.0), math.log(12.0)))
    raw_draws = jax.random.uniform(key_raw, (SUBBANDS, NZ, NZ), jnp.float32, 0.5, 1.5)
    paired = 0.5 * (raw_draws + jnp.swapaxes(raw_draws, 1, 2))
    diag_terms = jax.random.uniform(key_diag, (SUBBANDS, NZ), jnp.float32, 1.0, 2.0)
    identity_mat = jnp.eye(NZ, dtype=jnp.float32)
    band_numbers = jnp.arange(SUBBANDS)
    band_levels = jnp.minimum(band_numbers // 3 + 1, LEVELS).astype(jnp.float32)
    scales = jnp.reshape(jnp.exp2(band_levels) / 6.0, (SUBBANDS, 1, 1))
    matrix = identity_mat * diag_terms[:, :, None] + (1.0 - identity_mat) * 0.5 * jnp.exp(-distance / lengths) * paired
    return scales * matrix / (1.0 + lengths)


def block_levels(own_key, shape, cuts, smallest, high):
    gain, own = 1.0, jax.random.fold_in(own_key, 6)
    for axis_at, shards_of in cuts:
        steps = jnp.exp(jax.random.uniform(jax.random.fold_in(own, axis_at), (shards_of,), jnp.float32, smallest / len(cuts), high / len(cuts)))
        gain = gain * jnp.repeat(steps, shape[axis_at] // shards_of).reshape([-1 if axis == axis_at else 1 for axis in range(len(shape))])
    return gain


def scatter_about(own_key, extent, scale, bound, cuts=(), kind=jnp.bfloat16):
    entries = scale * jax.random.normal(own_key, extent, jnp.float32)
    if cuts:
        entries = entries * block_levels(own_key, extent, cuts, -0.22, 0.18)
    return jnp.clip(entries, -bound, bound).astype(kind)


def setup_inputs(seed: int = 0) -> dict:
    arg_keys = jax.random.split(jax.random.key(seed), 3)
    return {
        "increment": scatter_about(arg_keys[0], (MEMBERS, NZ, NX, NY), 1.0, 6.0, ((2, 8), (3, 4)), jnp.float32),
        "covariances": draw_covariances(jax.random.fold_in(arg_keys[2], 71), 0),
    }


LOW_TAPS = (0.2303778133088964, 0.7148465705529154, 0.6308807679298587, -0.0279837694168599,
            -0.1870348117190931, 0.0308413818355607, 0.0328830116668852, -0.0105974017850690)
HIGH_TAPS = (-0.0105974017850690, -0.0328830116668852, 0.0308413818355607, 0.1870348117190931,
             -0.0279837694168599, -0.6308807679298587, 0.7148465705529154, -0.2303778133088964)


def nothing(values):
    return jnp.zeros_like(values)


def split_axis(values, ahead_cells, along):
    extended = jnp.concatenate([values, ahead_cells], axis=along)
    count = values.shape[along] // 2
    smooth = None
    detail = None
    for j in range(8):
        strided = lax.slice_in_dim(extended, j, j + 2 * count - 1, stride=2, axis=along)
        if j == 0:
            smooth = LOW_TAPS[j] * strided
            detail = HIGH_TAPS[j] * strided
        else:
            smooth = smooth + LOW_TAPS[j] * strided
            detail = detail + HIGH_TAPS[j] * strided
    return smooth, detail


def upsample(joined, along):
    woven_pair = jnp.stack((joined, jnp.zeros_like(joined)), axis=along + 1)
    new_shape = list(joined.shape)
    new_shape[along] = new_shape[along] * 2
    spread = jnp.reshape(woven_pair, tuple(new_shape))
    lead_zero = jnp.zeros_like(lax.slice_in_dim(spread, 0, 1, axis=along))
    return jnp.concatenate([lead_zero, spread], axis=along)


def merge_axis(smooth, detail, behind_smooth, behind_detail, along):
    padded_smooth = upsample(jnp.concatenate([behind_smooth, smooth], axis=along), along)
    padded_detail = upsample(jnp.concatenate([behind_detail, detail], axis=along), along)
    length = 2 * smooth.shape[along]
    summed = None
    for j in range(8):
        part_smooth = lax.slice_in_dim(padded_smooth, 7 - j, 7 - j + length, axis=along)
        part_detail = lax.slice_in_dim(padded_detail, 7 - j, 7 - j + length, axis=along)
        term = LOW_TAPS[j] * part_smooth + HIGH_TAPS[j] * part_detail
        summed = term if j == 0 else summed + term
    return summed


def analyse(approx, fetch_rows, fetch_cols):
    ahead_rows = fetch_rows(approx[:, :, :6, :])
    low_x, high_x = split_axis(approx, ahead_rows, 2)
    fetched = fetch_cols(jnp.stack((low_x[..., :6], high_x[..., :6])))
    smooth_smooth, smooth_detail = split_axis(low_x, fetched[0], 3)
    detail_smooth, detail_detail = split_axis(high_x, fetched[1], 3)
    return smooth_smooth, (smooth_detail, detail_smooth, detail_detail)


def combine_level(smooth_smooth, details, fetch_cols, fetch_rows):
    smooth_detail, detail_smooth, detail_detail = details
    behind = fetch_cols(jnp.stack((smooth_smooth[..., -3:], smooth_detail[..., -3:],
                                   detail_smooth[..., -3:], detail_detail[..., -3:])))
    low_x = merge_axis(smooth_smooth, smooth_detail, behind[0], behind[1], 3)
    high_x = merge_axis(detail_smooth, detail_detail, behind[2], behind[3], 3)
    back_rows = fetch_rows(jnp.stack((low_x[:, :, -3:, :], high_x[:, :, -3:, :])))
    return merge_axis(low_x, high_x, back_rows[0], back_rows[1], 2)


def covary(coeffs, matrix):
    return jnp.einsum('zw,mwxy->mzxy', matrix, coeffs, precision=lax.Precision.HIGHEST)


def reference(increment, covariances):
    approx = increment
    stored = []
    for level_index in range(LEVELS):
        approx, details = analyse(approx, nothing, nothing)
        stored.append(details)
    result = covary(approx, covariances[3 * LEVELS])
    for level_index in reversed(range(LEVELS)):
        details = stored[level_index]
        mixed_bands = tuple(covary(details[band_index], covariances[3 * level_index + band_index])
                            for band_index in range(3))
        result = combine_level(result, mixed_bands, nothing, nothing)
    return result
```

```python
import functools

import jax
import jax.numpy as jnp
from jax import lax
from jax.experimental import pallas as pl
from jax.experimental.pallas import tpu as pltpu
from jax.sharding import PartitionSpec as P

LEVELS = 6
HANDOVER = 4
LANES = 128
COLS = 8
AHEAD = 6
BACK = {1: 4, 2: 6, 3: 6, 4: 6, 5: 6, 6: 6}
SENT = {1: 3, 2: 5, 3: 6}
MESH = pl.DeviceIdType.MESH

LOW_TAPS = (
    0.2303778133088964,
    0.7148465705529155,
    0.6308807679298587,
    -0.0279837694168599,
    -0.1870348117190931,
    0.0308413818355607,
    0.0328830116668852,
    -0.010597401785069,
)
HIGH_TAPS = (
    -0.010597401785069,
    -0.0328830116668852,
    0.0308413818355607,
    0.1870348117190931,
    -0.0279837694168599,
    -0.6308807679298587,
    0.7148465705529154,
    -0.2303778133088964,
)


def rows_loop(first, last, body):
    def step(r, carry):
        body(r)
        return carry

    lax.fori_loop(first, last, step, 0)


def split_rows(source, work, rows, cols):
    def body(k):
        smooth = detail = None
        for j in range(8):
            row = source[2 * k + j, 0:cols, :]
            if j == 0:
                smooth, detail = LOW_TAPS[j] * row, HIGH_TAPS[j] * row
            else:
                smooth, detail = smooth + LOW_TAPS[j] * row, detail + HIGH_TAPS[j] * row
        work[0, k, 0:cols, :] = smooth
        work[1, k, 0:cols, :] = detail

    rows_loop(0, rows, body)


def split_cols(work, rows, half, put):
    def body(k):
        for side in range(2):
            smooth = detail = None
            for j in range(8):
                part = work[side, k, pl.ds(j, half, stride=2), :]
                if j == 0:
                    smooth, detail = LOW_TAPS[j] * part, HIGH_TAPS[j] * part
                else:
                    smooth, detail = smooth + LOW_TAPS[j] * part, detail + HIGH_TAPS[j] * part
            put(side, k, smooth, detail)

    rows_loop(0, rows, body)


def halves(values):
    upper = values.astype(jnp.bfloat16)
    lower = (values - upper.astype(jnp.float32)).astype(jnp.bfloat16)
    return upper, lower


def product(values, upper, lower):
    first, second = halves(values)
    dot = functools.partial(jnp.dot, preferred_element_type=jnp.float32)
    return dot(first, upper) + (dot(second, upper) + dot(first, lower))


def mix(ref, band, cov, index, row0, rows, col0, cols):
    upper, lower = halves(cov[index])
    chunk = 1
    for c in range(1, rows + 1):
        if rows % c == 0 and c * cols <= 512:
            chunk = c

    def body(r):
        at = (band, pl.ds(row0 + r * chunk, chunk), slice(col0, col0 + cols), slice(None))
        values = ref[at].reshape(chunk * cols, LANES)
        ref[at] = product(values, upper, lower).reshape(chunk, cols, LANES)

    rows_loop(0, rows // chunk, body)


def merge_level(smooth, bands, work, out, back, first_row, rows, cols, out_cols, out_rows):
    count = cols + out_cols // 2
    start = COLS - out_cols // 2

    def along_y(r):
        for side in range(2):
            if side == 0:
                left, right = smooth.at[r], bands.at[0, r]
            else:
                left, right = bands.at[1, r], bands.at[2, r]
            even = odd = None
            for t in range(4):
                s = left[start - t:start - t + count, :]
                d = right[start - t:start - t + count, :]
                e = LOW_TAPS[2 * t] * s + HIGH_TAPS[2 * t] * d
                o = LOW_TAPS[2 * t + 1] * s + HIGH_TAPS[2 * t + 1] * d
                even, odd = (e, o) if t == 0 else (even + e, odd + o)
            work[side, r, pl.ds(0, count, stride=2), :] = even
            work[side, r, pl.ds(1, count, stride=2), :] = odd

    rows_loop(first_row, back + rows, along_y)
    width = 2 * cols + out_cols

    def along_x(n):
        even = odd = None
        for t in range(4):
            at = n - out_rows // 2 - t + back
            s = work[0, at, 0:width, :]
            d = work[1, at, 0:width, :]
            e = LOW_TAPS[2 * t] * s + HIGH_TAPS[2 * t] * d
            o = LOW_TAPS[2 * t + 1] * s + HIGH_TAPS[2 * t + 1] * d
            even, odd = (e, o) if t == 0 else (even + e, odd + o)
        out[2 * n, 0:width, :] = even
        out[2 * n + 1, 0:width, :] = odd

    rows_loop(0, rows + out_rows // 2, along_x)


def fill(ref):
    ref[...] = jnp.zeros(ref.shape, jnp.float32)


def kernel(nx, ny, X, Y, back_x, back_y, inc, cov, out, *scratch):
    (a0, a1, a2, a3, m1, m2, m3, s4, m4, g4, e4, e5, top, m5, m6, r6, r5, r4, r4l, r3, r2, r1,
     work, load_sem, a_send, a_recv, m_send, m_recv, s_send, s_recv, g_send, g_recv) = scratch
    approx = (a0, a1, a2, a3)
    mixed = {1: m1, 2: m2, 3: m3}
    gx, gy = lax.axis_index("gx"), lax.axis_index("gy")
    total = nx * ny
    me = gx * ny + gy
    X4, Y4 = X[4], Y[4]

    load = pltpu.make_async_copy(inc, a0.at[0:X[0], 0:Y[0]], load_sem)
    load.start()

    def place(o):
        other = lax.rem(me + o, total)
        return (lax.div(other, ny), lax.rem(other, ny))

    barrier = pltpu.get_barrier_semaphore()

    def greet(o):
        pl.semaphore_signal(barrier, inc=1, device_id=place(o), device_id_type=MESH)

    rows_loop(1, total, greet)
    pl.semaphore_wait(barrier, total - 1)

    sends = []

    def move(source, target, send_sem, recv_sem, dx, dy):
        def copy():
            return pltpu.make_async_remote_copy(
                src_ref=source, dst_ref=target, send_sem=send_sem, recv_sem=recv_sem,
                device_id=(gx + dx, gy + dy), device_id_type=MESH)

        def inside(px, py):
            terms = []
            if dx:
                terms += [px >= 0, px < nx]
            if dy:
                terms += [py >= 0, py < ny]
            return functools.reduce(jnp.logical_and, terms)

        gives, takes = inside(gx + dx, gy + dy), inside(gx - dx, gy - dy)

        @pl.when(gives)
        def _():
            copy().start()

        def sent():
            @pl.when(gives)
            def _():
                copy().wait_send()

        sends.append(sent)

        @pl.when(jnp.logical_not(takes))
        def _():
            fill(target)

        def arrive():
            @pl.when(takes)
            def _():
                copy().wait_recv()

        return arrive

    def send_ahead(level):
        ref, n, w = approx[level], X[level], Y[level]
        src = inc if level == 0 else ref
        own = ((slice(0, AHEAD), slice(0, w)), (slice(0, n), slice(0, COLS)), (slice(0, AHEAD), slice(0, COLS)))
        put = ((slice(n, n + AHEAD), slice(0, w)), (slice(0, n), slice(w, w + COLS)),
               (slice(n, n + AHEAD), slice(w, w + COLS)))
        way = ((-1, 0), (0, -1), (-1, -1))
        return [move(src.at[own[i]], ref.at[put[i]], a_send.at[3 * level + i], a_recv.at[3 * level + i], *way[i])
                for i in range(3)]

    def send_back(level):
        ref, n, w, b, s = mixed[level], X[level], Y[level], BACK[level], SENT[level]
        every = slice(0, 3)
        own = ((every, slice(b + n - s, b + n), slice(COLS, COLS + w)),
               (every, slice(b, b + n), slice(w, w + COLS)),
               (every, slice(b + n - s, b + n), slice(w, w + COLS)))
        put = ((every, slice(b - s, b), slice(COLS, COLS + w)),
               (every, slice(b, b + n), slice(0, COLS)),
               (every, slice(b - s, b), slice(0, COLS)))
        way = ((1, 0), (0, 1), (1, 1))
        base = 3 * (level - 1)
        return [move(ref.at[own[i]], ref.at[put[i]], m_send.at[base + i], m_recv.at[base + i], *way[i])
                for i in range(3)]

    arrivals = send_ahead(0)
    load.wait()
    late = {}
    for level in range(1, HANDOVER + 1):
        for arrive in arrivals:
            arrive()
        rows, cols = X[level], Y[level]
        split_rows(approx[level - 1], work, rows, Y[level - 1] + COLS)
        if level < HANDOVER:
            target, bands, b = approx[level], mixed[level], BACK[level]

            def put(side, k, smooth, detail):
                if side == 0:
                    target[k, 0:cols, :] = smooth
                    bands[0, b + k, COLS:COLS + cols, :] = detail
                else:
                    bands[1, b + k, COLS:COLS + cols, :] = smooth
                    bands[2, b + k, COLS:COLS + cols, :] = detail

            split_cols(work, rows, cols, put)
            arrivals = send_ahead(level)
            for band in range(3):
                mix(bands, band, cov, 3 * (level - 1) + band, b, rows, COLS, cols)
            late[level] = send_back(level)
        else:
            own4 = s4.at[0]
            if Y4 != COLS:
                fill(own4)
                fill(g4.at[me])

            def put(side, k, smooth, detail):
                if side == 0:
                    g4[me, k, 0:cols, :] = smooth
                    own4[0, k, 0:cols, :] = detail
                else:
                    own4[1, k, 0:cols, :] = smooth
                    own4[2, k, 0:cols, :] = detail

            split_cols(work, rows, cols, put)

    def spread(o):
        return pltpu.make_async_remote_copy(
            src_ref=g4.at[me], dst_ref=g4.at[me], send_sem=g_send.at[o], recv_sem=g_recv.at[o],
            device_id=place(o), device_id_type=MESH)

    def landed(o):
        return pltpu.make_async_remote_copy(
            src_ref=g4.at[me], dst_ref=g4.at[lax.rem(me + total - o, total)],
            send_sem=g_send.at[o], recv_sem=g_recv.at[o], device_id=place(o), device_id_type=MESH)

    rows_loop(1, total, lambda o: spread(o).start())

    for band in range(3):
        mix(s4.at[0], band, cov, 3 * (HANDOVER - 1) + band, 0, X4, 0, COLS)
    late4 = []
    for dx in range(back_x + 1):
        for dy in range(back_y + 1):
            if dx or dy:
                slot = dx * (back_y + 1) + dy
                late4.append(move(s4.at[0], s4.at[slot], s_send.at[slot], s_recv.at[slot], dx, dy))

    for ref in (e4, e5, m5, m6, r6):
        fill(ref)
    rows_loop(1, total, lambda o: landed(o).wait_recv())

    def assemble(px):
        for py in range(ny):
            for k in range(X4):
                e4[px * X4 + k, py * Y4:(py + 1) * Y4, :] = g4[px * ny + py, k, 0:Y4, :]

    rows_loop(0, nx, assemble)

    for level, source, target, bands in ((5, e4, e5, m5), (6, e5, top, m6)):
        rows, cols = X[level], Y[level]
        b = BACK[level]
        split_rows(source, work, rows, 2 * cols + COLS)

        def put(side, k, smooth, detail, target=target, bands=bands, b=b, cols=cols):
            if side == 0:
                if target is top:
                    r6[b + k, COLS:COLS + cols, :] = smooth
                else:
                    target[k, 0:cols, :] = smooth
                bands[0, b + k, COLS:COLS + cols, :] = detail
            else:
                bands[1, b + k, COLS:COLS + cols, :] = smooth
                bands[2, b + k, COLS:COLS + cols, :] = detail

        split_cols(work, rows, cols, put)
        for band in range(3):
            mix(bands, band, cov, 3 * (level - 1) + band, b, rows, COLS, cols)
    top[0] = r6[...]
    mix(top, 0, cov, 3 * LEVELS, BACK[6], X[6], COLS, Y[6])
    merge_level(top.at[0], m6, work, r5, BACK[6], 0, X[6], Y[6], COLS, BACK[5])
    merge_level(r5, m5, work, r4, BACK[5], 0, X[5], Y[5], COLS, BACK[4])

    for py in range(ny):
        @pl.when(gy == py)
        def _():
            def body(r):
                r4l[r, :, :] = r4[gx * X4 + r, py * Y4:py * Y4 + COLS + Y4, :]

            rows_loop(0, BACK[4] + X4, body)

    for arrive in late4:
        arrive()
    for dx in range(back_x + 1):
        for dy in range(back_y + 1):
            slot = dx * (back_y + 1) + dy
            row, col = BACK[4] - dx * X4, COLS - dy * Y4
            m4[:, row:row + X4, col:col + Y4, :] = s4[slot, :, :, 0:Y4, :]

    merge_level(r4l, m4, work, r3, BACK[4], 0, X4, Y4, COLS, BACK[3])
    for level, source, target in ((3, r3, r2), (2, r2, r1), (1, r1, out)):
        for arrive in late[level]:
            arrive()
        final = level == 1
        merge_level(source, mixed[level], work, target, BACK[level], BACK[level] - SENT[level], X[level], Y[level],
                    0 if final else COLS, 0 if final else BACK[level - 1])

    for sent in sends:
        sent()
    rows_loop(1, total, lambda o: spread(o).wait_send())


def per_device(nx, ny, increment, covariances):
    members, heights, block_x, block_y = increment.shape
    bands = covariances.shape[0]
    X = [block_x >> l for l in range(HANDOVER + 1)]
    Y = [block_y >> l for l in range(HANDOVER + 1)]
    wide_x, wide_y = nx * X[4], ny * Y[4]
    X += [wide_x // 2, wide_x // 4]
    Y += [wide_y // 2, wide_y // 4]
    back_x, back_y = BACK[4] // X[4], COLS // Y[4]
    extra = LANES - heights
    field = jnp.pad(jnp.transpose(increment[0], (1, 2, 0)), ((0, 0), (0, 0), (0, extra)))
    turned = jnp.pad(jnp.transpose(covariances, (0, 2, 1)), ((0, 0), (0, extra), (0, extra)))

    f32 = functools.partial(pltpu.VMEM, dtype=jnp.float32)

    def ahead(l):
        return f32((X[l] + AHEAD, Y[l] + COLS, LANES))

    def behind(l):
        return f32((BACK[l] + X[l], COLS + Y[l], LANES))

    def three(l):
        return f32((3, BACK[l] + X[l], COLS + Y[l], LANES))

    slots = (back_x + 1) * (back_y + 1)
    work_rows = max(X[1] + BACK[1], X[5] + BACK[5])
    work_cols = max(Y[0], wide_y) + COLS
    dma = pltpu.SemaphoreType.DMA
    scratch = [
        ahead(0), ahead(1), ahead(2), ahead(3),
        three(1), three(2), three(3),
        f32((slots, 3, X[4], COLS, LANES)), three(4),
        f32((nx * ny, X[4], COLS, LANES)),
        f32((wide_x + AHEAD, wide_y + COLS, LANES)), ahead(5),
        f32((1, BACK[6] + X[6], COLS + Y[6], LANES)),
        three(5), three(6), behind(6), behind(5),
        f32((BACK[4] + wide_x, COLS + wide_y, LANES)),
        behind(4), behind(3), behind(2), behind(1),
        f32((2, work_rows, work_cols, LANES)),
        dma, dma((12,)), dma((12,)), dma((9,)), dma((9,)), dma((slots,)), dma((slots,)),
        dma((nx * ny,)), dma((nx * ny,)),
    ]
    result = pl.pallas_call(
        functools.partial(kernel, nx, ny, X, Y, back_x, back_y),
        out_shape=jax.ShapeDtypeStruct((block_x, block_y, LANES), jnp.float32),
        in_specs=[pl.BlockSpec(memory_space=pl.ANY), pl.BlockSpec(memory_space=pltpu.VMEM)],
        out_specs=pl.BlockSpec(memory_space=pltpu.VMEM),
        scratch_shapes=scratch,
        compiler_params=pltpu.CompilerParams(
            collective_id=0, has_side_effects=True, vmem_limit_bytes=48 * 1024 * 1024),
    )(field, turned)
    return jnp.transpose(result[:, :, :heights], (2, 0, 1))[None]


def solution(mesh):
    nx, ny = mesh.shape["gx"], mesh.shape["gy"]
    placed = (P(None, None, "gx", "gy"), P())
    return jax.shard_map(
        functools.partial(per_device, nx, ny), mesh=mesh, in_specs=placed,
        out_specs=P(None, None, "gx", "gy"), check_vma=False)
```

```python
import functools

import jax
import jax.numpy as jnp
from jax import lax
from jax.experimental import pallas as pl
from jax.experimental.pallas import tpu as pltpu
from jax.sharding import PartitionSpec as P

LEVELS = 6
HANDOVER = 4
LANES = 128
COLS = 8
AHEAD = 6
BACK = {1: 4, 2: 6, 3: 6, 4: 6, 5: 6, 6: 6}
SENT = {1: 3, 2: 5, 3: 6}
MESH = pl.DeviceIdType.MESH

LOW_TAPS = (
    0.2303778133088964,
    0.7148465705529155,
    0.6308807679298587,
    -0.0279837694168599,
    -0.1870348117190931,
    0.0308413818355607,
    0.0328830116668852,
    -0.010597401785069,
)
HIGH_TAPS = (
    -0.010597401785069,
    -0.0328830116668852,
    0.0308413818355607,
    0.1870348117190931,
    -0.0279837694168599,
    -0.6308807679298587,
    0.7148465705529154,
    -0.2303778133088964,
)


def rows_loop(first, last, body):
    def step(r, carry):
        body(r)
        return carry

    lax.fori_loop(first, last, step, 0)


def split_rows(source, work, rows, cols):
    def body(k):
        smooth = detail = None
        for j in range(8):
            row = source[2 * k + j, 0:cols, :]
            if j == 0:
                smooth, detail = LOW_TAPS[j] * row, HIGH_TAPS[j] * row
            else:
                smooth, detail = smooth + LOW_TAPS[j] * row, detail + HIGH_TAPS[j] * row
        work[0, k, 0:cols, :] = smooth
        work[1, k, 0:cols, :] = detail

    rows_loop(0, rows, body)


def split_cols(work, rows, half, put):
    def body(k):
        for side in range(2):
            smooth = detail = None
            for j in range(8):
                part = work[side, k, pl.ds(j, half, stride=2), :]
                if j == 0:
                    smooth, detail = LOW_TAPS[j] * part, HIGH_TAPS[j] * part
                else:
                    smooth, detail = smooth + LOW_TAPS[j] * part, detail + HIGH_TAPS[j] * part
            put(side, k, smooth, detail)

    rows_loop(0, rows, body)


def halves(values):
    upper = values.astype(jnp.bfloat16)
    lower = (values - upper.astype(jnp.float32)).astype(jnp.bfloat16)
    return upper, lower


def product(values, upper, lower):
    first, second = halves(values)
    dot = functools.partial(jnp.dot, preferred_element_type=jnp.float32)
    return dot(first, upper) + (dot(second, upper) + dot(first, lower))


def mix(ref, band, cov, index, row0, rows, col0, cols):
    upper, lower = halves(cov[index])
    chunk = 1
    for c in range(1, rows + 1):
        if rows % c == 0 and c * cols <= 512:
            chunk = c

    def body(r):
        at = (band, pl.ds(row0 + r * chunk, chunk), slice(col0, col0 + cols), slice(None))
        values = ref[at].reshape(chunk * cols, LANES)
        ref[at] = product(values, upper, lower).reshape(chunk, cols, LANES)

    rows_loop(0, rows // chunk, body)


def merge_level(smooth, bands, work, out, back, first_row, rows, cols, out_cols, out_rows):
    count = cols + out_cols // 2
    start = COLS - out_cols // 2

    def along_y(r):
        for side in range(2):
            if side == 0:
                left, right = smooth.at[r], bands.at[0, r]
            else:
                left, right = bands.at[1, r], bands.at[2, r]
            even = odd = None
            for t in range(4):
                s = left[start - t:start - t + count, :]
                d = right[start - t:start - t + count, :]
                e = LOW_TAPS[2 * t] * s + HIGH_TAPS[2 * t] * d
                o = LOW_TAPS[2 * t + 1] * s + HIGH_TAPS[2 * t + 1] * d
                even, odd = (e, o) if t == 0 else (even + e, odd + o)
            work[side, r, pl.ds(0, count, stride=2), :] = even
            work[side, r, pl.ds(1, count, stride=2), :] = odd

    rows_loop(first_row, back + rows, along_y)
    width = 2 * cols + out_cols

    def along_x(n):
        even = odd = None
        for t in range(4):
            at = n - out_rows // 2 - t + back
            s = work[0, at, 0:width, :]
            d = work[1, at, 0:width, :]
            e = LOW_TAPS[2 * t] * s + HIGH_TAPS[2 * t] * d
            o = LOW_TAPS[2 * t + 1] * s + HIGH_TAPS[2 * t + 1] * d
            even, odd = (e, o) if t == 0 else (even + e, odd + o)
        out[2 * n, 0:width, :] = even
        out[2 * n + 1, 0:width, :] = odd

    rows_loop(0, rows + out_rows // 2, along_x)


def turn(ref, row, steps, planes):
    slab = ref.reshape(planes * steps, ref.shape[2])[pl.ds(row, planes, stride=steps), :]
    return jnp.concatenate([slab, jnp.zeros((LANES - planes, slab.shape[1]), jnp.float32)]).T


def fill(ref):
    ref[...] = jnp.zeros(ref.shape, jnp.float32)


def kernel(nx, ny, X, Y, back_x, back_y, inc, cov, out, *scratch):
    (raw, raw_ahead, a0, a1, a2, a3, m1, m2, m3, s4, m4, g4, e4, e5, top, m5, m6, r6, r5, r4, r4l, r3, r2, r1,
     work, load_sem, a_send, a_recv, m_send, m_recv, s_send, s_recv, g_send, g_recv, pair_send, pair_recv) = scratch
    approx = (a0, a1, a2, a3)
    mixed = {1: m1, 2: m2, 3: m3}
    gx, gy = lax.axis_index("gx"), lax.axis_index("gy")
    total = nx * ny
    me = gx * ny + gy
    X4, Y4 = X[4], Y[4]

    heights, planes = inc.shape[0], raw.shape[0]
    chips, wide = total // 2, ny // 2
    chip, core = gx * wide + lax.div(gy, 2), lax.rem(gy, 2)

    load = pltpu.make_async_copy(inc, raw.at[0:heights], load_sem)
    load.start()

    def place(o):
        other = lax.rem(me + o, total)
        return (lax.div(other, ny), lax.rem(other, ny))

    barrier = pltpu.get_barrier_semaphore()

    def greet(o):
        pl.semaphore_signal(barrier, inc=1, device_id=place(o), device_id_type=MESH)

    rows_loop(1, total, greet)
    if planes > heights:
        fill(raw.at[heights:planes])
        fill(raw_ahead.at[heights:planes])
    pl.semaphore_wait(barrier, total - 1)

    sends = []

    def move(source, target, send_sem, recv_sem, dx, dy, absent=None, present=None):
        def copy():
            return pltpu.make_async_remote_copy(
                src_ref=source, dst_ref=target, send_sem=send_sem, recv_sem=recv_sem,
                device_id=(gx + dx, gy + dy), device_id_type=MESH)

        def inside(px, py):
            terms = []
            if dx:
                terms += [px >= 0, px < nx]
            if dy:
                terms += [py >= 0, py < ny]
            return functools.reduce(jnp.logical_and, terms)

        gives, takes = inside(gx + dx, gy + dy), inside(gx - dx, gy - dy)

        @pl.when(gives)
        def _():
            copy().start()

        def sent():
            @pl.when(gives)
            def _():
                copy().wait_send()

        sends.append(sent)

        @pl.when(jnp.logical_not(takes))
        def _():
            (absent or (lambda: fill(target)))()

        def arrive():
            @pl.when(takes)
            def _():
                copy().wait_recv()
                if present:
                    present()

        return arrive

    def send_ahead(level):
        ref, n, w = approx[level], X[level], Y[level]
        own = ((slice(0, AHEAD), slice(0, w)), (slice(0, n), slice(0, COLS)), (slice(0, AHEAD), slice(0, COLS)))
        put = ((slice(n, n + AHEAD), slice(0, w)), (slice(0, n), slice(w, w + COLS)),
               (slice(n, n + AHEAD), slice(w, w + COLS)))
        way = ((-1, 0), (0, -1), (-1, -1))
        return [move(ref.at[own[i]], ref.at[put[i]], a_send.at[3 * level + i], a_recv.at[3 * level + i], *way[i])
                for i in range(1 if level == 0 else 0, 3)]

    def send_back(level):
        ref, n, w, b, s = mixed[level], X[level], Y[level], BACK[level], SENT[level]
        every = slice(0, 3)
        own = ((every, slice(b + n - s, b + n), slice(COLS, COLS + w)),
               (every, slice(b, b + n), slice(w, w + COLS)),
               (every, slice(b + n - s, b + n), slice(w, w + COLS)))
        put = ((every, slice(b - s, b), slice(COLS, COLS + w)),
               (every, slice(b, b + n), slice(0, COLS)),
               (every, slice(b - s, b), slice(0, COLS)))
        way = ((1, 0), (0, 1), (1, 1))
        base = 3 * (level - 1)
        return [move(ref.at[own[i]], ref.at[put[i]], m_send.at[base + i], m_recv.at[base + i], *way[i])
                for i in range(3)]

    def turn_ahead():
        for r in range(AHEAD):
            a0[X[0] + r, 0:Y[0], :] = turn(raw_ahead, r, COLS, planes)

    first = move(inc.at[:, 0:AHEAD, :], raw_ahead.at[0:heights, 0:AHEAD, :], a_send.at[0], a_recv.at[0], -1, 0,
                 lambda: fill(a0.at[X[0]:X[0] + AHEAD, 0:Y[0]]), turn_ahead)
    load.wait()

    def turn_own(r):
        a0[r, 0:Y[0], :] = turn(raw, r, X[0], planes)

    rows_loop(0, X[0], turn_own)
    arrivals = send_ahead(0) + [first]
    late = {}
    for level in range(1, HANDOVER + 1):
        for arrive in arrivals:
            arrive()
        rows, cols = X[level], Y[level]
        split_rows(approx[level - 1], work, rows, Y[level - 1] + COLS)
        if level < HANDOVER:
            target, bands, b = approx[level], mixed[level], BACK[level]

            def put(side, k, smooth, detail):
                if side == 0:
                    target[k, 0:cols, :] = smooth
                    bands[0, b + k, COLS:COLS + cols, :] = detail
                else:
                    bands[1, b + k, COLS:COLS + cols, :] = smooth
                    bands[2, b + k, COLS:COLS + cols, :] = detail

            split_cols(work, rows, cols, put)
            arrivals = send_ahead(level)
            for band in range(3):
                mix(bands, band, cov, 3 * (level - 1) + band, b, rows, COLS, cols)
            late[level] = send_back(level)
        else:
            own4 = s4.at[0]
            if Y4 != COLS:
                fill(own4)
                fill(g4.at[core, chip])

            def put(side, k, smooth, detail):
                if side == 0:
                    g4[core, chip, k, 0:cols, :] = smooth
                    own4[0, k, 0:cols, :] = detail
                else:
                    own4[1, k, 0:cols, :] = smooth
                    own4[2, k, 0:cols, :] = detail

            split_cols(work, rows, cols, put)

    def spread(o):
        other = lax.rem(chip + o, chips)
        return pltpu.make_async_remote_copy(
            src_ref=g4.at[core, chip], dst_ref=g4.at[core, chip], send_sem=g_send.at[o], recv_sem=g_recv.at[o],
            device_id=(lax.div(other, wide), 2 * lax.rem(other, wide) + core), device_id_type=MESH)

    def landed(o):
        return pltpu.make_async_remote_copy(
            src_ref=g4.at[core, chip], dst_ref=g4.at[core, lax.rem(chip + chips - o, chips)],
            send_sem=g_send.at[o], recv_sem=g_recv.at[o], device_id=(gx, gy + 1 - 2 * core), device_id_type=MESH)

    def pair(side):
        return pltpu.make_async_remote_copy(
            src_ref=g4.at[side], dst_ref=g4.at[side], send_sem=pair_send, recv_sem=pair_recv,
            device_id=(gx, gy + 1 - 2 * core), device_id_type=MESH)

    rows_loop(1, chips, lambda o: spread(o).start())

    for band in range(3):
        mix(s4.at[0], band, cov, 3 * (HANDOVER - 1) + band, 0, X4, 0, COLS)
    late4 = []
    for dx in range(back_x + 1):
        for dy in range(back_y + 1):
            if dx or dy:
                slot = dx * (back_y + 1) + dy
                late4.append(move(s4.at[0], s4.at[slot], s_send.at[slot], s_recv.at[slot], dx, dy))

    for ref in (e4, e5, m5, m6, r6):
        fill(ref)
    rows_loop(1, chips, lambda o: landed(o).wait_recv())
    pair(core).start()
    pair(1 - core).wait_recv()

    def assemble(px):
        for py in range(ny):
            for k in range(X4):
                e4[px * X4 + k, py * Y4:(py + 1) * Y4, :] = g4[py % 2, px * wide + py // 2, k, 0:Y4, :]

    rows_loop(0, nx, assemble)

    for level, source, target, bands in ((5, e4, e5, m5), (6, e5, top, m6)):
        rows, cols = X[level], Y[level]
        b = BACK[level]
        split_rows(source, work, rows, 2 * cols + COLS)

        def put(side, k, smooth, detail, target=target, bands=bands, b=b, cols=cols):
            if side == 0:
                if target is top:
                    r6[b + k, COLS:COLS + cols, :] = smooth
                else:
                    target[k, 0:cols, :] = smooth
                bands[0, b + k, COLS:COLS + cols, :] = detail
            else:
                bands[1, b + k, COLS:COLS + cols, :] = smooth
                bands[2, b + k, COLS:COLS + cols, :] = detail

        split_cols(work, rows, cols, put)
        for band in range(3):
            mix(bands, band, cov, 3 * (level - 1) + band, b, rows, COLS, cols)
    top[0] = r6[...]
    mix(top, 0, cov, 3 * LEVELS, BACK[6], X[6], COLS, Y[6])
    merge_level(top.at[0], m6, work, r5, BACK[6], 0, X[6], Y[6], COLS, BACK[5])
    merge_level(r5, m5, work, r4, BACK[5], 0, X[5], Y[5], COLS, BACK[4])

    for py in range(ny):
        @pl.when(gy == py)
        def _():
            def body(r):
                r4l[r, :, :] = r4[gx * X4 + r, py * Y4:py * Y4 + COLS + Y4, :]

            rows_loop(0, BACK[4] + X4, body)

    for arrive in late4:
        arrive()
    for dx in range(back_x + 1):
        for dy in range(back_y + 1):
            slot = dx * (back_y + 1) + dy
            row, col = BACK[4] - dx * X4, COLS - dy * Y4
            m4[:, row:row + X4, col:col + Y4, :] = s4[slot, :, :, 0:Y4, :]

    merge_level(r4l, m4, work, r3, BACK[4], 0, X4, Y4, COLS, BACK[3])
    for level, source, target in ((3, r3, r2), (2, r2, r1), (1, r1, out)):
        for arrive in late[level]:
            arrive()
        final = level == 1
        merge_level(source, mixed[level], work, target, BACK[level], BACK[level] - SENT[level], X[level], Y[level],
                    0 if final else COLS, 0 if final else BACK[level - 1])

    for sent in sends:
        sent()
    rows_loop(1, chips, lambda o: spread(o).wait_send())
    pair(core).wait_send()


def per_device(nx, ny, increment, covariances):
    members, heights, block_x, block_y = increment.shape
    bands = covariances.shape[0]
    X = [block_x >> l for l in range(HANDOVER + 1)]
    Y = [block_y >> l for l in range(HANDOVER + 1)]
    wide_x, wide_y = nx * X[4], ny * Y[4]
    X += [wide_x // 2, wide_x // 4]
    Y += [wide_y // 2, wide_y // 4]
    back_x, back_y = BACK[4] // X[4], COLS // Y[4]
    extra = LANES - heights
    planes = -(-heights // 8) * 8
    turned = jnp.pad(jnp.transpose(covariances, (0, 2, 1)), ((0, 0), (0, extra), (0, extra)))

    f32 = functools.partial(pltpu.VMEM, dtype=jnp.float32)

    def ahead(l):
        return f32((X[l] + AHEAD, Y[l] + COLS, LANES))

    def behind(l):
        return f32((BACK[l] + X[l], COLS + Y[l], LANES))

    def three(l):
        return f32((3, BACK[l] + X[l], COLS + Y[l], LANES))

    slots = (back_x + 1) * (back_y + 1)
    work_rows = max(X[1] + BACK[1], X[5] + BACK[5])
    work_cols = max(Y[0], wide_y) + COLS
    dma = pltpu.SemaphoreType.DMA
    scratch = [
        f32((planes, block_x, block_y)), f32((planes, COLS, block_y)),
        ahead(0), ahead(1), ahead(2), ahead(3),
        three(1), three(2), three(3),
        f32((slots, 3, X[4], COLS, LANES)), three(4),
        f32((2, nx * ny // 2, X[4], COLS, LANES)),
        f32((wide_x + AHEAD, wide_y + COLS, LANES)), ahead(5),
        f32((1, BACK[6] + X[6], COLS + Y[6], LANES)),
        three(5), three(6), behind(6), behind(5),
        f32((BACK[4] + wide_x, COLS + wide_y, LANES)),
        behind(4), behind(3), behind(2), behind(1),
        f32((2, work_rows, work_cols, LANES)),
        dma, dma((12,)), dma((12,)), dma((9,)), dma((9,)), dma((slots,)), dma((slots,)),
        dma((nx * ny // 2,)), dma((nx * ny // 2,)), dma, dma,
    ]
    result = pl.pallas_call(
        functools.partial(kernel, nx, ny, X, Y, back_x, back_y),
        out_shape=jax.ShapeDtypeStruct((block_x, block_y, LANES), jnp.float32),
        in_specs=[pl.BlockSpec(memory_space=pl.ANY), pl.BlockSpec(memory_space=pltpu.VMEM)],
        out_specs=pl.BlockSpec(memory_space=pltpu.VMEM),
        scratch_shapes=scratch,
        compiler_params=pltpu.CompilerParams(
            collective_id=0, has_side_effects=True, vmem_limit_bytes=48 * 1024 * 1024),
    )(increment[0], turned)
    return jnp.transpose(result[:, :, :heights], (2, 0, 1))[None]


def solution(mesh):
    nx, ny = mesh.shape["gx"], mesh.shape["gy"]
    placed = (P(None, None, "gx", "gy"), P())
    return jax.shard_map(
        functools.partial(per_device, nx, ny), mesh=mesh, in_specs=placed,
        out_specs=P(None, None, "gx", "gy"), check_vma=False)
```

```python
import functools

import jax
import jax.numpy as jnp
from jax import lax
from jax.experimental import pallas as pl
from jax.experimental.pallas import tpu as pltpu
from jax.sharding import PartitionSpec as P

LEVELS = 6
HANDOVER = 4
LANES = 128
UNROLL_A, UNROLL_B, UNROLL_C, UNROLL_T = 2, 4, 4, 8
COLS = 8
AHEAD = 6
BACK = {1: 4, 2: 6, 3: 6, 4: 6, 5: 6, 6: 6}
SENT = {1: 3, 2: 5, 3: 6}
MESH = pl.DeviceIdType.MESH

LOW_TAPS = (
    0.2303778133088964,
    0.7148465705529155,
    0.6308807679298587,
    -0.0279837694168599,
    -0.1870348117190931,
    0.0308413818355607,
    0.0328830116668852,
    -0.010597401785069,
)
HIGH_TAPS = (
    -0.010597401785069,
    -0.0328830116668852,
    0.0308413818355607,
    0.1870348117190931,
    -0.0279837694168599,
    -0.6308807679298587,
    0.7148465705529154,
    -0.2303778133088964,
)


def rows_loop(first, last, body, unroll=1):
    whole = (last - first) // unroll

    def step(r, carry):
        for u in range(unroll):
            body(first + r * unroll + u)
        return carry

    lax.fori_loop(0, whole, step, 0)
    for r in range(first + whole * unroll, last):
        body(r)


def split_rows(source, work, rows, cols):
    def body(k):
        smooth = detail = None
        for j in range(8):
            row = source[2 * k + j, 0:cols, :]
            if j == 0:
                smooth, detail = LOW_TAPS[j] * row, HIGH_TAPS[j] * row
            else:
                smooth, detail = smooth + LOW_TAPS[j] * row, detail + HIGH_TAPS[j] * row
        work[0, k, 0:cols, :] = smooth
        work[1, k, 0:cols, :] = detail

    rows_loop(0, rows, body, UNROLL_A)


def split_cols(work, rows, half, put):
    def body(k):
        for side in range(2):
            smooth = detail = None
            for j in range(8):
                part = work[side, k, pl.ds(j, half, stride=2), :]
                if j == 0:
                    smooth, detail = LOW_TAPS[j] * part, HIGH_TAPS[j] * part
                else:
                    smooth, detail = smooth + LOW_TAPS[j] * part, detail + HIGH_TAPS[j] * part
            put(side, k, smooth, detail)

    rows_loop(0, rows, body, UNROLL_B)


def halves(values):
    upper = values.astype(jnp.bfloat16)
    lower = (values - upper.astype(jnp.float32)).astype(jnp.bfloat16)
    return upper, lower


def product(values, upper, lower):
    first, second = halves(values)
    dot = functools.partial(
        lax.dot_general, dimension_numbers=(((1,), (1,)), ((), ())), preferred_element_type=jnp.float32)
    return dot(first, upper) + (dot(second, upper) + dot(first, lower))


def mix(ref, band, cov, index, row0, rows, col0, cols):
    upper, lower = halves(cov[index])
    heights = cov.shape[1]
    chunk = 1
    for c in range(1, rows + 1):
        if rows % c == 0 and c * cols <= 512:
            chunk = c

    def body(r):
        at = (band, pl.ds(row0 + r * chunk, chunk), slice(col0, col0 + cols), slice(0, heights))
        values = ref[at].reshape(chunk * cols, heights)
        ref[at] = product(values, upper, lower).reshape(chunk, cols, heights)

    rows_loop(0, rows // chunk, body, UNROLL_C)


def merge_level(smooth, bands, work, out, back, first_row, rows, cols, out_cols, out_rows):
    count = cols + out_cols // 2
    start = COLS - out_cols // 2

    def along_y(r):
        for side in range(2):
            if side == 0:
                left, right = smooth.at[r], bands.at[0, r]
            else:
                left, right = bands.at[1, r], bands.at[2, r]
            even = odd = None
            for t in range(4):
                s = left[start - t:start - t + count, :]
                d = right[start - t:start - t + count, :]
                e = LOW_TAPS[2 * t] * s + HIGH_TAPS[2 * t] * d
                o = LOW_TAPS[2 * t + 1] * s + HIGH_TAPS[2 * t + 1] * d
                even, odd = (e, o) if t == 0 else (even + e, odd + o)
            work[side, r, pl.ds(0, count, stride=2), :] = even
            work[side, r, pl.ds(1, count, stride=2), :] = odd

    rows_loop(first_row, back + rows, along_y, UNROLL_B)
    width = 2 * cols + out_cols

    def along_x(n):
        even = odd = None
        for t in range(4):
            at = n - out_rows // 2 - t + back
            s = work[0, at, 0:width, :]
            d = work[1, at, 0:width, :]
            e = LOW_TAPS[2 * t] * s + HIGH_TAPS[2 * t] * d
            o = LOW_TAPS[2 * t + 1] * s + HIGH_TAPS[2 * t + 1] * d
            even, odd = (e, o) if t == 0 else (even + e, odd + o)
        out[2 * n, 0:width, :] = even[:, :out.shape[2]]
        out[2 * n + 1, 0:width, :] = odd[:, :out.shape[2]]

    rows_loop(0, rows + out_rows // 2, along_x, UNROLL_A)


def turn(ref, row, steps, planes):
    slab = ref.reshape(planes * steps, ref.shape[2])[pl.ds(row, planes, stride=steps), :]
    return jnp.concatenate([slab, jnp.zeros((LANES - planes, slab.shape[1]), jnp.float32)]).T


def lane_of(rows):
    return lax.broadcasted_iota(jnp.int32, (rows, LANES), 1)


def pack(values, heights):
    flat = values.reshape(-1, LANES)
    quarter, piece = flat.shape[0] // 4, -(-heights // 3)
    kept = LANES - piece
    lane, last = lane_of(quarter), flat[3 * quarter:]
    return jnp.stack([
        jnp.where(lane < kept, flat[i * quarter:(i + 1) * quarter], pltpu.roll(last, (kept - piece * i) % LANES, 1))
        for i in range(3)])


def unpack(packed, heights, shape):
    quarter, piece = packed.shape[1], -(-heights // 3)
    kept = LANES - piece
    lane, last = lane_of(quarter), jnp.zeros((quarter, LANES), jnp.float32)
    for i in range(3):
        back = pltpu.roll(packed[i], (LANES + piece * i - kept) % LANES, 1)
        last = jnp.where((lane >= piece * i) & (lane < piece * (i + 1)), back, last)
    first = [jnp.where(lane < kept, packed[i], 0.0) for i in range(3)]
    return jnp.concatenate(first + [last]).reshape(shape)


def fill(ref):
    ref[...] = jnp.zeros(ref.shape, jnp.float32)


def kernel(nx, ny, X, Y, back_x, back_y, inc, cov, out, *scratch):
    (raw, raw_ahead, a0, a1, a2, a3, m1, m2, m3, s4, m4, g4, e4, e5, top, m5, m6, r6, r5, r4, r4l, r3, r2, r1,
     work, load_sem, a_send, a_recv, m_send, m_recv, s_send, s_recv, g_send, g_recv, pair_send, pair_recv, *boxes) = scratch
    approx = (a0, a1, a2, a3)
    mixed = {1: m1, 2: m2, 3: m3}
    gx, gy = lax.axis_index("gx"), lax.axis_index("gy")
    total = nx * ny
    me = gx * ny + gy
    X4, Y4 = X[4], Y[4]

    heights, planes = inc.shape[0], raw.shape[0]
    chips, wide = total // 2, ny // 2
    chip, core = gx * wide + lax.div(gy, 2), lax.rem(gy, 2)

    load = pltpu.make_async_copy(inc, raw.at[0:heights], load_sem)
    load.start()

    def place(o):
        other = lax.rem(me + o, total)
        return (lax.div(other, ny), lax.rem(other, ny))

    barrier = pltpu.get_barrier_semaphore()

    def greet(o):
        pl.semaphore_signal(barrier, inc=1, device_id=place(o), device_id_type=MESH)

    rows_loop(1, total, greet)
    if planes > heights:
        fill(raw.at[heights:planes])
        fill(raw_ahead.at[heights:planes])
    pl.semaphore_wait(barrier, total - 1)

    sends = []

    def move(source, target, send_sem, recv_sem, dx, dy, absent=None, present=None):
        def copy():
            return pltpu.make_async_remote_copy(
                src_ref=source, dst_ref=target, send_sem=send_sem, recv_sem=recv_sem,
                device_id=(gx + dx, gy + dy), device_id_type=MESH)

        def inside(px, py):
            terms = []
            if dx:
                terms += [px >= 0, px < nx]
            if dy:
                terms += [py >= 0, py < ny]
            return functools.reduce(jnp.logical_and, terms)

        gives, takes = inside(gx + dx, gy + dy), inside(gx - dx, gy - dy)

        @pl.when(gives)
        def _():
            copy().start()

        def sent():
            @pl.when(gives)
            def _():
                copy().wait_send()

        sends.append(sent)

        @pl.when(jnp.logical_not(takes))
        def _():
            (absent or (lambda: fill(target)))()

        def arrive():
            @pl.when(takes)
            def _():
                copy().wait_recv()
                if present:
                    present()

        return arrive

    def move_packed(box, source, target, send_sem, recv_sem, dx, dy):
        box[0] = pack(source[...], heights)

        def present():
            target[...] = unpack(box[1], heights, target.shape)

        return move(box.at[0], box.at[1], send_sem, recv_sem, dx, dy, lambda: fill(target), present)

    def send_ahead(level):
        ref, n, w = approx[level], X[level], Y[level]
        own = ((slice(0, AHEAD), slice(0, w)), (slice(0, n), slice(0, COLS)), (slice(0, AHEAD), slice(0, COLS)))
        put = ((slice(n, n + AHEAD), slice(0, w)), (slice(0, n), slice(w, w + COLS)),
               (slice(n, n + AHEAD), slice(w, w + COLS)))
        way = ((-1, 0), (0, -1), (-1, -1))
        steps = [move(ref.at[own[i]], ref.at[put[i]], a_send.at[3 * level + i], a_recv.at[3 * level + i], *way[i])
                 for i in range(1, 3)]
        if level:
            steps.append(move_packed(boxes[level - 1], ref.at[own[0]], ref.at[put[0]],
                                     a_send.at[3 * level], a_recv.at[3 * level], *way[0]))
        return steps

    def send_back(level):
        ref, n, w, b, s = mixed[level], X[level], Y[level], BACK[level], SENT[level]
        every = slice(0, 3)
        own = ((every, slice(b + n - s, b + n), slice(COLS, COLS + w)),
               (every, slice(b, b + n), slice(w, w + COLS)),
               (every, slice(b + n - s, b + n), slice(w, w + COLS)))
        put = ((every, slice(b - s, b), slice(COLS, COLS + w)),
               (every, slice(b, b + n), slice(0, COLS)),
               (every, slice(b - s, b), slice(0, COLS)))
        way = ((1, 0), (0, 1), (1, 1))
        base = 3 * (level - 1)
        return [move_packed(boxes[2 + level], ref.at[own[0]], ref.at[put[0]], m_send.at[base], m_recv.at[base], *way[0])
                ] + [move(ref.at[own[i]], ref.at[put[i]], m_send.at[base + i], m_recv.at[base + i], *way[i])
                     for i in range(1, 3)]

    def turn_ahead():
        for r in range(AHEAD):
            a0[X[0] + r, 0:Y[0], :] = turn(raw_ahead, r, COLS, planes)

    first = move(inc.at[:, 0:AHEAD, :], raw_ahead.at[0:heights, 0:AHEAD, :], a_send.at[0], a_recv.at[0], -1, 0,
                 lambda: fill(a0.at[X[0]:X[0] + AHEAD, 0:Y[0]]), turn_ahead)
    load.wait()

    def turn_own(r):
        a0[r, 0:Y[0], :] = turn(raw, r, X[0], planes)

    rows_loop(0, X[0], turn_own, UNROLL_T)
    arrivals = send_ahead(0) + [first]
    late = {}
    for level in range(1, HANDOVER + 1):
        for arrive in arrivals:
            arrive()
        rows, cols = X[level], Y[level]
        split_rows(approx[level - 1], work, rows, Y[level - 1] + COLS)
        if level < HANDOVER:
            target, bands, b = approx[level], mixed[level], BACK[level]

            def put(side, k, smooth, detail):
                if side == 0:
                    target[k, 0:cols, :] = smooth
                    bands[0, b + k, COLS:COLS + cols, :] = detail
                else:
                    bands[1, b + k, COLS:COLS + cols, :] = smooth
                    bands[2, b + k, COLS:COLS + cols, :] = detail

            split_cols(work, rows, cols, put)
            arrivals = send_ahead(level)
            for band in range(3):
                mix(bands, band, cov, 3 * (level - 1) + band, b, rows, COLS, cols)
            late[level] = send_back(level)
        else:
            own4 = s4.at[0]
            if Y4 != COLS:
                fill(own4)
                fill(g4.at[core, chip])

            def put(side, k, smooth, detail):
                if side == 0:
                    g4[core, chip, k, 0:cols, :] = smooth
                    own4[0, k, 0:cols, :] = detail
                else:
                    own4[1, k, 0:cols, :] = smooth
                    own4[2, k, 0:cols, :] = detail

            split_cols(work, rows, cols, put)

    def spread(o):
        other = lax.rem(chip + o, chips)
        return pltpu.make_async_remote_copy(
            src_ref=g4.at[core, chip], dst_ref=g4.at[core, chip], send_sem=g_send.at[o], recv_sem=g_recv.at[o],
            device_id=(lax.div(other, wide), 2 * lax.rem(other, wide) + core), device_id_type=MESH)

    def landed(o):
        return pltpu.make_async_remote_copy(
            src_ref=g4.at[core, chip], dst_ref=g4.at[core, lax.rem(chip + chips - o, chips)],
            send_sem=g_send.at[o], recv_sem=g_recv.at[o], device_id=(gx, gy + 1 - 2 * core), device_id_type=MESH)

    def pair(side):
        return pltpu.make_async_remote_copy(
            src_ref=g4.at[side], dst_ref=g4.at[side], send_sem=pair_send, recv_sem=pair_recv,
            device_id=(gx, gy + 1 - 2 * core), device_id_type=MESH)

    rows_loop(1, chips, lambda o: spread(o).start())

    for band in range(3):
        mix(s4.at[0], band, cov, 3 * (HANDOVER - 1) + band, 0, X4, 0, COLS)
    late4 = []
    for dx in range(back_x + 1):
        for dy in range(back_y + 1):
            if dx or dy:
                slot = dx * (back_y + 1) + dy
                late4.append(move(s4.at[0], s4.at[slot], s_send.at[slot], s_recv.at[slot], dx, dy))

    for ref in (e4, e5, m5, m6, r6):
        fill(ref)
    rows_loop(1, chips, lambda o: landed(o).wait_recv())
    pair(core).start()
    pair(1 - core).wait_recv()

    def assemble(px):
        for py in range(ny):
            for k in range(X4):
                e4[px * X4 + k, py * Y4:(py + 1) * Y4, :] = g4[py % 2, px * wide + py // 2, k, 0:Y4, :]

    rows_loop(0, nx, assemble)

    for level, source, target, bands in ((5, e4, e5, m5), (6, e5, top, m6)):
        rows, cols = X[level], Y[level]
        b = BACK[level]
        split_rows(source, work, rows, 2 * cols + COLS)

        def put(side, k, smooth, detail, target=target, bands=bands, b=b, cols=cols):
            if side == 0:
                if target is top:
                    r6[b + k, COLS:COLS + cols, :] = smooth
                else:
                    target[k, 0:cols, :] = smooth
                bands[0, b + k, COLS:COLS + cols, :] = detail
            else:
                bands[1, b + k, COLS:COLS + cols, :] = smooth
                bands[2, b + k, COLS:COLS + cols, :] = detail

        split_cols(work, rows, cols, put)
        for band in range(3):
            mix(bands, band, cov, 3 * (level - 1) + band, b, rows, COLS, cols)
    top[0] = r6[...]
    mix(top, 0, cov, 3 * LEVELS, BACK[6], X[6], COLS, Y[6])
    merge_level(top.at[0], m6, work, r5, BACK[6], 0, X[6], Y[6], COLS, BACK[5])
    merge_level(r5, m5, work, r4, BACK[5], 0, X[5], Y[5], COLS, BACK[4])

    for py in range(ny):
        @pl.when(gy == py)
        def _():
            def body(r):
                r4l[r, :, :] = r4[gx * X4 + r, py * Y4:py * Y4 + COLS + Y4, :]

            rows_loop(0, BACK[4] + X4, body)

    for arrive in late4:
        arrive()
    for dx in range(back_x + 1):
        for dy in range(back_y + 1):
            slot = dx * (back_y + 1) + dy
            row, col = BACK[4] - dx * X4, COLS - dy * Y4
            m4[:, row:row + X4, col:col + Y4, :] = s4[slot, :, :, 0:Y4, :]

    merge_level(r4l, m4, work, r3, BACK[4], 0, X4, Y4, COLS, BACK[3])
    for level, source, target in ((3, r3, r2), (2, r2, r1), (1, r1, out)):
        for arrive in late[level]:
            arrive()
        final = level == 1
        merge_level(source, mixed[level], work, target, BACK[level], BACK[level] - SENT[level], X[level], Y[level],
                    0 if final else COLS, 0 if final else BACK[level - 1])

    for sent in sends:
        sent()
    rows_loop(1, chips, lambda o: spread(o).wait_send())
    pair(core).wait_send()


def per_device(nx, ny, increment, covariances):
    members, heights, block_x, block_y = increment.shape
    bands = covariances.shape[0]
    X = [block_x >> l for l in range(HANDOVER + 1)]
    Y = [block_y >> l for l in range(HANDOVER + 1)]
    wide_x, wide_y = nx * X[4], ny * Y[4]
    X += [wide_x // 2, wide_x // 4]
    Y += [wide_y // 2, wide_y // 4]
    back_x, back_y = BACK[4] // X[4], COLS // Y[4]
    planes = -(-heights // 8) * 8

    f32 = functools.partial(pltpu.VMEM, dtype=jnp.float32)

    def ahead(l):
        return f32((X[l] + AHEAD, Y[l] + COLS, LANES))

    def behind(l):
        return f32((BACK[l] + X[l], COLS + Y[l], LANES))

    def three(l):
        return f32((3, BACK[l] + X[l], COLS + Y[l], LANES))

    def box(rows, l):
        return f32((2, 3, rows * Y[l] // 4, LANES))

    slots = (back_x + 1) * (back_y + 1)
    work_rows = max(X[1] + BACK[1], X[5] + BACK[5])
    work_cols = max(Y[0], wide_y) + COLS
    dma = pltpu.SemaphoreType.DMA
    scratch = [
        f32((planes, block_x, block_y)), f32((planes, COLS, block_y)),
        ahead(0), ahead(1), ahead(2), ahead(3),
        three(1), three(2), three(3),
        f32((slots, 3, X[4], COLS, LANES)), three(4),
        f32((2, nx * ny // 2, X[4], COLS, LANES)),
        f32((wide_x + AHEAD, wide_y + COLS, LANES)), ahead(5),
        f32((1, BACK[6] + X[6], COLS + Y[6], LANES)),
        three(5), three(6), behind(6), behind(5),
        f32((BACK[4] + wide_x, COLS + wide_y, LANES)),
        behind(4), behind(3), behind(2), behind(1),
        f32((2, work_rows, work_cols, LANES)),
        dma, dma((12,)), dma((12,)), dma((9,)), dma((9,)), dma((slots,)), dma((slots,)),
        dma((nx * ny // 2,)), dma((nx * ny // 2,)), dma, dma,
        box(AHEAD, 1), box(AHEAD, 2), box(AHEAD, 3), box(3 * SENT[1], 1), box(3 * SENT[2], 2), box(3 * SENT[3], 3),
    ]
    result = pl.pallas_call(
        functools.partial(kernel, nx, ny, X, Y, back_x, back_y),
        out_shape=jax.ShapeDtypeStruct((block_x, block_y, heights), jnp.float32),
        in_specs=[pl.BlockSpec(memory_space=pl.ANY), pl.BlockSpec(memory_space=pltpu.VMEM)],
        out_specs=pl.BlockSpec(memory_space=pltpu.VMEM),
        scratch_shapes=scratch,
        compiler_params=pltpu.CompilerParams(
            collective_id=0, has_side_effects=True, vmem_limit_bytes=48 * 1024 * 1024),
    )(increment[0], covariances)
    return jnp.transpose(result, (2, 0, 1))[None]


def solution(mesh):
    nx, ny = mesh.shape["gx"], mesh.shape["gy"]
    placed = (P(None, None, "gx", "gy"), P())
    return jax.shard_map(
        functools.partial(per_device, nx, ny), mesh=mesh, in_specs=placed,
        out_specs=P(None, None, "gx", "gy"), check_vma=False)
```

```python
import functools

import jax
import jax.numpy as jnp
from jax import lax
from jax.experimental import pallas as pl
from jax.experimental.pallas import tpu as pltpu
from jax.sharding import PartitionSpec as P

LEVELS = 6
HANDOVER = 4
LANES = 128
UNROLL_A, UNROLL_B, UNROLL_C, UNROLL_T = 2, 4, 4, 8
COLS = 8
AHEAD = 6
BACK = {1: 4, 2: 6, 3: 6, 4: 6, 5: 6, 6: 6}
SENT = {1: 3, 2: 5, 3: 6}
MESH = pl.DeviceIdType.MESH

LOW_TAPS = (
    0.2303778133088964,
    0.7148465705529155,
    0.6308807679298587,
    -0.0279837694168599,
    -0.1870348117190931,
    0.0308413818355607,
    0.0328830116668852,
    -0.010597401785069,
)
HIGH_TAPS = (
    -0.010597401785069,
    -0.0328830116668852,
    0.0308413818355607,
    0.1870348117190931,
    -0.0279837694168599,
    -0.6308807679298587,
    0.7148465705529154,
    -0.2303778133088964,
)


def rows_loop(first, last, body, unroll=1):
    whole = (last - first) // unroll

    def step(r, carry):
        for u in range(unroll):
            body(first + r * unroll + u)
        return carry

    lax.fori_loop(0, whole, step, 0)
    for r in range(first + whole * unroll, last):
        body(r)


def split_rows(source, work, rows, first, cols):
    def body(k):
        smooth = detail = None
        for j in range(8):
            row = source[2 * k + j, first:cols, :]
            if j == 0:
                smooth, detail = LOW_TAPS[j] * row, HIGH_TAPS[j] * row
            else:
                smooth, detail = smooth + LOW_TAPS[j] * row, detail + HIGH_TAPS[j] * row
        work[0, k, first:cols, :] = smooth
        work[1, k, first:cols, :] = detail

    rows_loop(0, rows, body, UNROLL_A)


def split_cols(work, rows, half, put):
    def body(k):
        for side in range(2):
            smooth = detail = None
            for j in range(8):
                part = work[side, k, pl.ds(j, half, stride=2), :]
                if j == 0:
                    smooth, detail = LOW_TAPS[j] * part, HIGH_TAPS[j] * part
                else:
                    smooth, detail = smooth + LOW_TAPS[j] * part, detail + HIGH_TAPS[j] * part
            put(side, k, smooth, detail)

    rows_loop(0, rows, body, UNROLL_B)


def halves(values):
    upper = values.astype(jnp.bfloat16)
    lower = (values - upper.astype(jnp.float32)).astype(jnp.bfloat16)
    return upper, lower


def product(values, upper, lower):
    first, second = halves(values)
    dot = functools.partial(
        lax.dot_general, dimension_numbers=(((1,), (1,)), ((), ())), preferred_element_type=jnp.float32)
    return dot(first, upper) + (dot(second, upper) + dot(first, lower))


def mix(ref, band, cov, index, row0, rows, col0, cols):
    upper, lower = halves(cov[index])
    heights = cov.shape[1]
    chunk = 1
    for c in range(1, rows + 1):
        if rows % c == 0 and c * cols <= 512:
            chunk = c

    def body(r):
        at = (band, pl.ds(row0 + r * chunk, chunk), slice(col0, col0 + cols), slice(0, heights))
        values = ref[at].reshape(chunk * cols, heights)
        ref[at] = product(values, upper, lower).reshape(chunk, cols, heights)

    rows_loop(0, rows // chunk, body, UNROLL_C)


def merge_level(smooth, bands, work, out, back, first_row, rows, cols, out_cols, out_rows):
    count = cols + out_cols // 2
    start = COLS - out_cols // 2

    def along_y(r):
        for side in range(2):
            if side == 0:
                left, right = smooth.at[r], bands.at[0, r]
            else:
                left, right = bands.at[1, r], bands.at[2, r]
            even = odd = None
            for t in range(4):
                s = left[start - t:start - t + count, :]
                d = right[start - t:start - t + count, :]
                e = LOW_TAPS[2 * t] * s + HIGH_TAPS[2 * t] * d
                o = LOW_TAPS[2 * t + 1] * s + HIGH_TAPS[2 * t + 1] * d
                even, odd = (e, o) if t == 0 else (even + e, odd + o)
            work[side, r, pl.ds(0, count, stride=2), :] = even
            work[side, r, pl.ds(1, count, stride=2), :] = odd

    rows_loop(first_row, back + rows, along_y, UNROLL_B)
    width = 2 * cols + out_cols

    def along_x(n):
        even = odd = None
        for t in range(4):
            at = n - out_rows // 2 - t + back
            s = work[0, at, 0:width, :]
            d = work[1, at, 0:width, :]
            e = LOW_TAPS[2 * t] * s + HIGH_TAPS[2 * t] * d
            o = LOW_TAPS[2 * t + 1] * s + HIGH_TAPS[2 * t + 1] * d
            even, odd = (e, o) if t == 0 else (even + e, odd + o)
        out[2 * n, 0:width, :] = even[:, :out.shape[2]]
        out[2 * n + 1, 0:width, :] = odd[:, :out.shape[2]]

    rows_loop(0, rows + out_rows // 2, along_x, UNROLL_A)


def turn(ref, row, steps, planes):
    slab = ref.reshape(planes * steps, ref.shape[2])[pl.ds(row, planes, stride=steps), :]
    return jnp.concatenate([slab, jnp.zeros((LANES - planes, slab.shape[1]), jnp.float32)]).T


def lane_of(rows):
    return lax.broadcasted_iota(jnp.int32, (rows, LANES), 1)


def pack(values, heights):
    flat = values.reshape(-1, LANES)
    quarter, piece = flat.shape[0] // 4, -(-heights // 3)
    kept = LANES - piece
    lane, last = lane_of(quarter), flat[3 * quarter:]
    return jnp.stack([
        jnp.where(lane < kept, flat[i * quarter:(i + 1) * quarter], pltpu.roll(last, (kept - piece * i) % LANES, 1))
        for i in range(3)])


def unpack(packed, heights, shape):
    quarter, piece = packed.shape[1], -(-heights // 3)
    kept = LANES - piece
    lane, last = lane_of(quarter), jnp.zeros((quarter, LANES), jnp.float32)
    for i in range(3):
        back = pltpu.roll(packed[i], (LANES + piece * i - kept) % LANES, 1)
        last = jnp.where((lane >= piece * i) & (lane < piece * (i + 1)), back, last)
    first = [jnp.where(lane < kept, packed[i], 0.0) for i in range(3)]
    return jnp.concatenate(first + [last]).reshape(shape)


def fill(ref):
    ref[...] = jnp.zeros(ref.shape, jnp.float32)


def kernel(nx, ny, X, Y, back_x, back_y, inc, cov, out, *scratch):
    (raw, raw_ahead, a0, a1, a2, a3, m1, m2, m3, s4, m4, g4, e4, e5, top, m5, m6, r6, r5, r4, r4l, r3, r2, r1,
     work, load_sem, a_send, a_recv, m_send, m_recv, s_send, s_recv, g_send, g_recv, pair_send, pair_recv, *boxes) = scratch
    approx = (a0, a1, a2, a3)
    mixed = {1: m1, 2: m2, 3: m3}
    gx, gy = lax.axis_index("gx"), lax.axis_index("gy")
    total = nx * ny
    me = gx * ny + gy
    X4, Y4 = X[4], Y[4]

    heights, planes = inc.shape[0], raw.shape[0]
    chips, wide = total // 2, ny // 2
    chip, core = gx * wide + lax.div(gy, 2), lax.rem(gy, 2)

    load = pltpu.make_async_copy(inc, raw.at[0:heights], load_sem)
    load.start()

    def place(o):
        other = lax.rem(me + o, total)
        return (lax.div(other, ny), lax.rem(other, ny))

    barrier = pltpu.get_barrier_semaphore()

    def greet(o):
        pl.semaphore_signal(barrier, inc=1, device_id=place(o), device_id_type=MESH)

    rows_loop(1, total, greet)
    if planes > heights:
        fill(raw.at[heights:planes])
        fill(raw_ahead.at[heights:planes])
    pl.semaphore_wait(barrier, total - 1)

    sends = []

    def move(source, target, send_sem, recv_sem, dx, dy, absent=None, present=None):
        def copy():
            return pltpu.make_async_remote_copy(
                src_ref=source, dst_ref=target, send_sem=send_sem, recv_sem=recv_sem,
                device_id=(gx + dx, gy + dy), device_id_type=MESH)

        def inside(px, py):
            terms = []
            if dx:
                terms += [px >= 0, px < nx]
            if dy:
                terms += [py >= 0, py < ny]
            return functools.reduce(jnp.logical_and, terms)

        gives, takes = inside(gx + dx, gy + dy), inside(gx - dx, gy - dy)

        @pl.when(gives)
        def _():
            copy().start()

        def sent():
            @pl.when(gives)
            def _():
                copy().wait_send()

        sends.append(sent)

        @pl.when(jnp.logical_not(takes))
        def _():
            (absent or (lambda: fill(target)))()

        def arrive():
            @pl.when(takes)
            def _():
                copy().wait_recv()
                if present:
                    present()

        return arrive

    def move_packed(box, source, target, send_sem, recv_sem, dx, dy):
        box[0] = pack(source[...], heights)

        def present():
            target[...] = unpack(box[1], heights, target.shape)

        return move(box.at[0], box.at[1], send_sem, recv_sem, dx, dy, lambda: fill(target), present)

    def send_ahead(level):
        ref, n, w = approx[level], X[level], Y[level]
        s = 3 * level
        cols = move(ref.at[0:n, 0:COLS], ref.at[0:n, w:w + COLS], a_send.at[s + 1], a_recv.at[s + 1], 0, -1)
        rows = None
        if level:
            rows = move_packed(boxes[level - 1], ref.at[0:AHEAD, 0:w], ref.at[n:n + AHEAD, 0:w],
                               a_send.at[s], a_recv.at[s], -1, 0)
        return rows, cols

    def corner_ahead(level):
        ref, n, w = approx[level], X[level], Y[level]
        s = 3 * level + 2
        return move(ref.at[n:n + AHEAD, 0:COLS], ref.at[n:n + AHEAD, w:w + COLS], a_send.at[s], a_recv.at[s], 0, -1)

    def send_back(level):
        ref, n, w, b, s = mixed[level], X[level], Y[level], BACK[level], SENT[level]
        k = 3 * (level - 1)
        rows = move_packed(boxes[2 + level], ref.at[:, b + n - s:b + n, COLS:COLS + w],
                           ref.at[:, b - s:b, COLS:COLS + w], m_send.at[k], m_recv.at[k], 1, 0)
        cols = move(ref.at[:, b:b + n, w:w + COLS], ref.at[:, b:b + n, 0:COLS], m_send.at[k + 1], m_recv.at[k + 1], 0, 1)
        return rows, cols

    def corner_back(level):
        ref, w, b, s = mixed[level], Y[level], BACK[level], SENT[level]
        k = 3 * (level - 1) + 2
        return move(ref.at[:, b - s:b, w:w + COLS], ref.at[:, b - s:b, 0:COLS], m_send.at[k], m_recv.at[k], 0, 1)

    def turn_ahead():
        for r in range(AHEAD):
            a0[X[0] + r, 0:Y[0], :] = turn(raw_ahead, r, COLS, planes)

    first = move(inc.at[:, 0:AHEAD, :], raw_ahead.at[0:heights, 0:AHEAD, :], a_send.at[0], a_recv.at[0], -1, 0,
                 lambda: fill(a0.at[X[0]:X[0] + AHEAD, 0:Y[0]]), turn_ahead)
    load.wait()

    def turn_own(r):
        a0[r, 0:Y[0], :] = turn(raw, r, X[0], planes)

    rows_loop(0, X[0], turn_own, UNROLL_T)
    arrivals = (first, send_ahead(0)[1])
    late = {}
    for level in range(1, HANDOVER + 1):
        rows, cols = X[level], Y[level]
        own = Y[level - 1]
        arrivals[0]()
        corner = corner_ahead(level - 1)
        split_rows(approx[level - 1], work, rows, 0, own)
        arrivals[1]()
        corner()
        split_rows(approx[level - 1], work, rows, own, own + COLS)
        if level < HANDOVER:
            target, bands, b = approx[level], mixed[level], BACK[level]

            def put(side, k, smooth, detail):
                if side == 0:
                    target[k, 0:cols, :] = smooth
                    bands[0, b + k, COLS:COLS + cols, :] = detail
                else:
                    bands[1, b + k, COLS:COLS + cols, :] = smooth
                    bands[2, b + k, COLS:COLS + cols, :] = detail

            split_cols(work, rows, cols, put)
            arrivals = send_ahead(level)
            for band in range(3):
                mix(bands, band, cov, 3 * (level - 1) + band, b, rows, COLS, cols)
            pass
        else:
            own4 = s4.at[0]
            if Y4 != COLS:
                fill(own4)
                fill(g4.at[core, chip])

            def put(side, k, smooth, detail):
                if side == 0:
                    g4[core, chip, k, 0:cols, :] = smooth
                    own4[0, k, 0:cols, :] = detail
                else:
                    own4[1, k, 0:cols, :] = smooth
                    own4[2, k, 0:cols, :] = detail

            split_cols(work, rows, cols, put)

    def spread(o):
        other = lax.rem(chip + o, chips)
        return pltpu.make_async_remote_copy(
            src_ref=g4.at[core, chip], dst_ref=g4.at[core, chip], send_sem=g_send.at[o], recv_sem=g_recv.at[o],
            device_id=(lax.div(other, wide), 2 * lax.rem(other, wide) + core), device_id_type=MESH)

    def landed(o):
        return pltpu.make_async_remote_copy(
            src_ref=g4.at[core, chip], dst_ref=g4.at[core, lax.rem(chip + chips - o, chips)],
            send_sem=g_send.at[o], recv_sem=g_recv.at[o], device_id=(gx, gy + 1 - 2 * core), device_id_type=MESH)

    def pair(side):
        return pltpu.make_async_remote_copy(
            src_ref=g4.at[side], dst_ref=g4.at[side], send_sem=pair_send, recv_sem=pair_recv,
            device_id=(gx, gy + 1 - 2 * core), device_id_type=MESH)

    rows_loop(1, chips, lambda o: spread(o).start())

    for band in range(3):
        mix(s4.at[0], band, cov, 3 * (HANDOVER - 1) + band, 0, X4, 0, COLS)
    def block(dx, dy):
        slot, source = dx * (back_y + 1) + dy, dx * (back_y + 1) if dy else 0
        return move(s4.at[source], s4.at[slot], s_send.at[slot], s_recv.at[slot], 0 if dy else dx, dy)

    behind_x = [block(dx, 0) for dx in range(1, back_x + 1)]
    late4 = [block(0, dy) for dy in range(1, back_y + 1)]

    for ref in (e4, e5, m5, m6, r6):
        fill(ref)
    for level in (3, 2, 1):
        late[level] = send_back(level)
    rows_loop(1, chips, lambda o: landed(o).wait_recv())
    pair(core).start()
    pair(1 - core).wait_recv()

    for dx in range(1, back_x + 1):
        behind_x[dx - 1]()
        late4 += [block(dx, dy) for dy in range(1, back_y + 1)]

    def assemble(px):
        for py in range(ny):
            for k in range(X4):
                e4[px * X4 + k, py * Y4:(py + 1) * Y4, :] = g4[py % 2, px * wide + py // 2, k, 0:Y4, :]

    rows_loop(0, nx, assemble)

    for level, source, target, bands in ((5, e4, e5, m5), (6, e5, top, m6)):
        rows, cols = X[level], Y[level]
        b = BACK[level]
        split_rows(source, work, rows, 0, 2 * cols + COLS)

        def put(side, k, smooth, detail, target=target, bands=bands, b=b, cols=cols):
            if side == 0:
                if target is top:
                    r6[b + k, COLS:COLS + cols, :] = smooth
                else:
                    target[k, 0:cols, :] = smooth
                bands[0, b + k, COLS:COLS + cols, :] = detail
            else:
                bands[1, b + k, COLS:COLS + cols, :] = smooth
                bands[2, b + k, COLS:COLS + cols, :] = detail

        split_cols(work, rows, cols, put)
        for band in range(3):
            mix(bands, band, cov, 3 * (level - 1) + band, b, rows, COLS, cols)
    top[0] = r6[...]
    mix(top, 0, cov, 3 * LEVELS, BACK[6], X[6], COLS, Y[6])
    merge_level(top.at[0], m6, work, r5, BACK[6], 0, X[6], Y[6], COLS, BACK[5])
    merge_level(r5, m5, work, r4, BACK[5], 0, X[5], Y[5], COLS, BACK[4])

    def forward(level):
        late[level][0]()
        late[level] = (late[level][1], corner_back(level))

    forward(3)
    for py in range(ny):
        @pl.when(gy == py)
        def _():
            def body(r):
                r4l[r, :, :] = r4[gx * X4 + r, py * Y4:py * Y4 + COLS + Y4, :]

            rows_loop(0, BACK[4] + X4, body)

    for arrive in late4:
        arrive()
    for dx in range(back_x + 1):
        for dy in range(back_y + 1):
            slot = dx * (back_y + 1) + dy
            row, col = BACK[4] - dx * X4, COLS - dy * Y4
            m4[:, row:row + X4, col:col + Y4, :] = s4[slot, :, :, 0:Y4, :]

    merge_level(r4l, m4, work, r3, BACK[4], 0, X4, Y4, COLS, BACK[3])
    for level, source, target in ((3, r3, r2), (2, r2, r1), (1, r1, out)):
        if level > 1:
            forward(level - 1)
        for arrive in late[level]:
            arrive()
        final = level == 1
        merge_level(source, mixed[level], work, target, BACK[level], BACK[level] - SENT[level], X[level], Y[level],
                    0 if final else COLS, 0 if final else BACK[level - 1])

    for sent in sends:
        sent()
    rows_loop(1, chips, lambda o: spread(o).wait_send())
    pair(core).wait_send()


def per_device(nx, ny, increment, covariances):
    members, heights, block_x, block_y = increment.shape
    bands = covariances.shape[0]
    X = [block_x >> l for l in range(HANDOVER + 1)]
    Y = [block_y >> l for l in range(HANDOVER + 1)]
    wide_x, wide_y = nx * X[4], ny * Y[4]
    X += [wide_x // 2, wide_x // 4]
    Y += [wide_y // 2, wide_y // 4]
    back_x, back_y = BACK[4] // X[4], COLS // Y[4]
    planes = -(-heights // 8) * 8

    f32 = functools.partial(pltpu.VMEM, dtype=jnp.float32)

    def ahead(l):
        return f32((X[l] + AHEAD, Y[l] + COLS, LANES))

    def behind(l):
        return f32((BACK[l] + X[l], COLS + Y[l], LANES))

    def three(l):
        return f32((3, BACK[l] + X[l], COLS + Y[l], LANES))

    def box(rows, l):
        return f32((2, 3, rows * Y[l] // 4, LANES))

    slots = (back_x + 1) * (back_y + 1)
    work_rows = max(X[1] + BACK[1], X[5] + BACK[5])
    work_cols = max(Y[0], wide_y) + COLS
    dma = pltpu.SemaphoreType.DMA
    scratch = [
        f32((planes, block_x, block_y)), f32((planes, COLS, block_y)),
        ahead(0), ahead(1), ahead(2), ahead(3),
        three(1), three(2), three(3),
        f32((slots, 3, X[4], COLS, LANES)), three(4),
        f32((2, nx * ny // 2, X[4], COLS, LANES)),
        f32((wide_x + AHEAD, wide_y + COLS, LANES)), ahead(5),
        f32((1, BACK[6] + X[6], COLS + Y[6], LANES)),
        three(5), three(6), behind(6), behind(5),
        f32((BACK[4] + wide_x, COLS + wide_y, LANES)),
        behind(4), behind(3), behind(2), behind(1),
        f32((2, work_rows, work_cols, LANES)),
        dma, dma((12,)), dma((12,)), dma((9,)), dma((9,)), dma((slots,)), dma((slots,)),
        dma((nx * ny // 2,)), dma((nx * ny // 2,)), dma, dma,
        box(AHEAD, 1), box(AHEAD, 2), box(AHEAD, 3), box(3 * SENT[1], 1), box(3 * SENT[2], 2), box(3 * SENT[3], 3),
    ]
    result = pl.pallas_call(
        functools.partial(kernel, nx, ny, X, Y, back_x, back_y),
        out_shape=jax.ShapeDtypeStruct((block_x, block_y, heights), jnp.float32),
        in_specs=[pl.BlockSpec(memory_space=pl.ANY), pl.BlockSpec(memory_space=pltpu.VMEM)],
        out_specs=pl.BlockSpec(memory_space=pltpu.VMEM),
        scratch_shapes=scratch,
        compiler_params=pltpu.CompilerParams(
            collective_id=0, has_side_effects=True, vmem_limit_bytes=48 * 1024 * 1024),
    )(increment[0], covariances)
    return jnp.transpose(result, (2, 0, 1))[None]


def solution(mesh):
    nx, ny = mesh.shape["gx"], mesh.shape["gy"]
    placed = (P(None, None, "gx", "gy"), P())
    return jax.shard_map(
        functools.partial(per_device, nx, ny), mesh=mesh, in_specs=placed,
        out_specs=P(None, None, "gx", "gy"), check_vma=False)
```
